32 devices in a mesh: grp: 4 (over z), shard: 2 (over x), tp: 4 (over y, core).
Axes of the slice: x: 2, y: 2, z: 4, core: 2. Of those that a mesh axis runs over, the one named last changes fastest.
Arguments:
- inner_weights: float32 [4, 2, 4096, 7168], P('grp', None, 'shard', 'tp'), may hold values from -6 to 6
- start_weights: float32 [2, 4096, 7168], P(None, 'shard', 'tp'), may hold values from -6 to 6
- momentum: float32 [2, 2, 4, 32, 64, 1792], P(None, None, None, ('grp', 'shard', 'tp')), may hold values from -6 to 6
Outputs:
- new_weights: float32 [2, 4096, 7168], P(None, 'shard', 'tp')
- new_momentum: float32 [2, 2, 4, 32, 64, 1792], P(None, None, None, ('grp', 'shard', 'tp'))
The draws below stay inside these ranges and needn't reach their ends.
All inputs are finite; a program needn't handle non-finite values.
Results may differ from the reference program's by a relative error of at most 0.00002.
Values sent between devices are 32-bit elements; how exact they have to be, the bound alone decides.
No kernel may reach another device: no remote copies, remote signals or barrier semaphores. Data moves between devices by JAX's collectives and lax.ppermute only.
A program may use at most 192 MiB of HBM per device.

```python
import jax
import jax.numpy as jnp

D = 4096
FF = 7168
QROWS = 64
N_GRP = 4
N_SHARD = 2
N_TP = 4
DEVICES = 32


def block_levels(stream_key, dims, shards, low, high):
    def one(axis_at, shards_of):
        draws = jax.random.uniform(jax.random.fold_in(jax.random.fold_in(stream_key, 6), axis_at), (shards_of,), jnp.float32, low / len(shards), high / len(shards))
        return jnp.repeat(jnp.exp(draws), dims[axis_at] // shards_of).reshape((-1,) + (1,) * (len(dims) - axis_at - 1))

    loudness = one(*shards[0])
    for cut in shards[1:]:
        loudness = loudness * one(*cut)
    return loudness


def noise(own_key, shape, spread, most, split=(), kind=jnp.bfloat16):
    factor_of = block_levels(own_key, shape, split, -0.22, 0.18) if split else 1.0
    drawn = jax.random.normal(own_key, shape, jnp.float32) * spread * factor_of
    return jnp.minimum(jnp.maximum(drawn, -most), most).astype(kind)


def setup_inputs(seed: int = 0) -> dict:
    splits = jax.random.split(jax.random.key(seed), 4)
    inner_weights = noise(splits[0], (N_GRP, 2, D, FF), 1.0, 6.0, ((0, 4), (2, 2), (3, 4)), jnp.float32)
    start_weights = noise(splits[1], (2, D, FF), 1.0, 6.0, ((1, 2), (2, 4)), jnp.float32)
    momentum = noise(splits[2], (2, N_SHARD, N_TP, DEVICES, QROWS, FF // N_TP), 1.0, 6.0, ((3, 32),), jnp.float32)
    return {"inner_weights": inner_weights, "start_weights": start_weights, "momentum": momentum}


OUTER_RATE = 0.7
MOMENTUM_COEF = 0.5


def reference(inner_weights, start_weights, momentum):
    summed = jnp.zeros(start_weights.shape, jnp.float32)
    for member in range(N_GRP):
        summed = summed + (start_weights - inner_weights[member])
    mean_diff = summed / N_GRP
    flat_diff = mean_diff.reshape(2, N_SHARD, DEVICES, QROWS, N_TP, FF // N_TP).transpose(0, 1, 4, 2, 3, 5)
    new_momentum = MOMENTUM_COEF * momentum + flat_diff
    flat_step = OUTER_RATE * (flat_diff + MOMENTUM_COEF * new_momentum)
    update = flat_step.transpose(0, 1, 3, 4, 2, 5).reshape(2, D, FF)
    new_weights = start_weights - update
    return new_weights, new_momentum
```

```python
import jax
import jax.numpy as jnp
from jax import lax
from jax.experimental import pallas as pl
from jax.sharding import PartitionSpec as P

OUTER_RATE = 0.7
MOMENTUM_COEF = 0.5
STEPS = 8


def blank(shape):
    return pl.pallas_call(
        lambda out: None,
        out_shape=jax.ShapeDtypeStruct(shape, jnp.float32),
        out_specs=pl.BlockSpec(memory_space=pl.ANY),
    )()


def body(inner_weights, start_weights, momentum):
    groups = lax.axis_size("grp")
    shards = lax.axis_size("shard")
    tp_size = lax.axis_size("tp")
    plane = shards * tp_size
    group = lax.axis_index("grp")
    place = lax.axis_index(("shard", "tp"))
    row_count, col_count = start_weights.shape[1:]
    q_rows = row_count // (groups * plane)
    steps = min(STEPS, plane)
    merge = plane // steps
    block = (q_rows, col_count)

    inner = inner_weights.reshape((2, groups, plane) + block)
    start = start_weights.reshape((2, groups, plane) + block)
    held = momentum.reshape((2, plane) + block)
    rightward = [(i, i + 1) for i in range(groups - 1)]
    leftward = [(i + 1, i) for i in range(groups - 1)]

    def lane(shift):
        return lax.rem(place + shift, plane)

    def cut(array, *at):
        return lax.dynamic_slice(array, at + (0, 0), (1,) * len(at) + block).reshape(block)

    def join(parts):
        return parts[0] if merge == 1 else jnp.concatenate(parts, axis=0)

    def parts_of(chunk):
        return [chunk[m * q_rows : (m + 1) * q_rows] for m in range(merge)]

    def rows_of(array, matrix, owner, step):
        return join([cut(array, matrix, owner, lane(step * merge + m)) for m in range(merge)])

    def own(matrix, owner, step):
        return rows_of(start, matrix, owner, step) - rows_of(inner, matrix, owner, step)

    def momentum_of(matrix, step):
        parts = []
        for m in range(merge):
            shift = step * merge + m
            part = cut(held, matrix, lane(plane - shift))
            if shift:
                part = lax.ppermute(part, ("shard", "tp"), [(i, (i - shift) % plane) for i in range(plane)])
            parts.append(part)
        return join(parts)

    new_weights = blank(start.shape)
    new_held = blank(held.shape)

    def write_weights(array, matrix, owner, step, update):
        for m, part in enumerate(parts_of(update)):
            at = (matrix, owner, lane(step * merge + m))
            array = lax.dynamic_update_slice(array, (cut(start, *at) - part)[None, None, None], at + (0, 0))
        return array

    def write_momentum(array, matrix, step, value):
        for m, part in enumerate(parts_of(value)):
            shift = step * merge + m
            if shift:
                part = lax.ppermute(part, ("shard", "tp"), [(i, (i + shift) % plane) for i in range(plane)])
            array = lax.dynamic_update_slice(array, part[None, None], (matrix, lane(plane - shift), 0, 0))
        return array

    moved = [[momentum_of(matrix, step) for step in range(steps)] for matrix in range(2)]
    zero = jnp.zeros((merge * q_rows, col_count), jnp.float32)
    from_left, from_right = [zero, zero], [zero, zero]
    arrived_left, arrived_right = [[], []], [[], []]

    for turn in range(steps + 1):
        for phase in range(1, groups + 1):
            for matrix in range(2):
                if turn == steps and phase == groups:
                    continue
                if phase < groups:
                    to_right, to_left = from_left[matrix], from_right[matrix]
                    if turn < steps:
                        right_owner = jnp.minimum(groups - phase + group, groups - 1)
                        left_owner = jnp.maximum(group - (groups - phase), 0)
                        to_right = jnp.where(group < phase, to_right + own(matrix, right_owner, turn), to_right)
                        to_left = jnp.where(
                            groups - 1 - group < phase, to_left + own(matrix, left_owner, turn), to_left
                        )
                else:
                    total = own(matrix, group, turn) + from_left[matrix] + from_right[matrix]
                    mean_diff = total / groups
                    new_momentum = MOMENTUM_COEF * moved[matrix][turn] + mean_diff
                    update = OUTER_RATE * (mean_diff + MOMENTUM_COEF * new_momentum)
                    new_held = write_momentum(new_held, matrix, turn, new_momentum)
                    new_weights = write_weights(new_weights, matrix, group, turn, update)
                    to_right = to_left = update
                if turn == steps and phase == groups - 1:
                    continue
                other = 1 - matrix
                to_right, to_left, from_left[other], from_right[other] = lax.optimization_barrier(
                    (to_right, to_left, from_left[other], from_right[other])
                )
                from_left[matrix] = lax.ppermute(to_right, "grp", rightward)
                from_right[matrix] = lax.ppermute(to_left, "grp", leftward)
                if phase == groups:
                    arrived_left[matrix], arrived_right[matrix] = [], []
                if phase == groups or turn > 0:
                    arrived_left[matrix].append(from_left[matrix])
                    arrived_right[matrix].append(from_right[matrix])
                    if len(arrived_left[matrix]) == groups - 1:
                        step = turn - 1
                        for hop in range(groups - 1):
                            update = jnp.where(
                                group > hop,
                                arrived_left[matrix][hop],
                                arrived_right[matrix][groups - 2 - hop],
                            )
                            owner = lax.rem(group + groups - 1 - hop, groups)
                            new_weights = write_weights(new_weights, matrix, owner, step, update)
    return (new_weights.reshape(start_weights.shape), new_held.reshape(momentum.shape))


def solution(mesh):
    in_specs = (
        P("grp", None, "shard", "tp"),
        P(None, "shard", "tp"),
        P(None, None, None, ("grp", "shard", "tp"), None, None),
    )
    out_specs = (P(None, "shard", "tp"), P(None, None, None, ("grp", "shard", "tp"), None, None))
    return jax.shard_map(body, mesh=mesh, in_specs=in_specs, out_specs=out_specs, check_vma=False)
```

```python
import jax
import jax.numpy as jnp
from jax import lax
from jax.experimental import pallas as pl
from jax.sharding import PartitionSpec as P

OUTER_RATE = 0.7
MOMENTUM_COEF = 0.5
STEPS = 8


def blank(shape):
    return pl.pallas_call(
        lambda out: None,
        out_shape=jax.ShapeDtypeStruct(shape, jnp.float32),
        out_specs=pl.BlockSpec(memory_space=pl.ANY),
    )()


def body(inner_weights, start_weights, momentum):
    groups = lax.axis_size("grp")
    shards = lax.axis_size("shard")
    tp_size = lax.axis_size("tp")
    plane = shards * tp_size
    group = lax.axis_index("grp")
    place = lax.axis_index(("shard", "tp"))
    row_count, col_count = start_weights.shape[1:]
    q_rows = row_count // (groups * plane)
    steps = min(STEPS, plane)
    merge = plane // steps
    block = (q_rows, col_count)

    inner = inner_weights.reshape((2, groups, plane) + block)
    start = start_weights.reshape((2, groups, plane) + block)
    held = momentum.reshape((2, plane) + block)
    rightward = [(i, i + 1) for i in range(groups - 1)]
    leftward = [(i + 1, i) for i in range(groups - 1)]

    def lane(shift):
        return lax.rem(place + shift, plane)

    def cut(array, *at):
        return lax.dynamic_slice(array, at + (0, 0), (1,) * len(at) + block).reshape(block)

    def join(parts):
        return parts[0] if merge == 1 else jnp.concatenate(parts, axis=0)

    def parts_of(chunk):
        return [chunk[m * q_rows : (m + 1) * q_rows] for m in range(merge)]

    def rows_of(array, matrix, owner, step):
        return join([cut(array, matrix, owner, lane(step * merge + m)) for m in range(merge)])

    def own(matrix, owner, step):
        return rows_of(start, matrix, owner, step) - rows_of(inner, matrix, owner, step)

    def rotate(part, shift):
        if shift % plane == 0:
            return part
        return lax.ppermute(part, ("shard", "tp"), [(i, (i + shift) % plane) for i in range(plane)])

    new_weights = blank(start.shape)
    new_held = blank(held.shape)

    def write_weights(array, matrix, owner, step, update):
        for m, part in enumerate(parts_of(update)):
            at = (matrix, owner, lane(step * merge + m))
            array = lax.dynamic_update_slice(array, (cut(start, *at) - part)[None, None, None], at + (0, 0))
        return array

    def after(first, *arrays):
        return lax.optimization_barrier((first, *arrays))[1:]

    order = [(turn + 1) % steps for turn in range(steps)]
    zero = jnp.zeros((merge * q_rows, col_count), jnp.float32)
    from_left, from_right = [zero, zero], [zero, zero]
    arrived_left, arrived_right = [[], []], [[], []]
    moved, outgoing, transit = {}, {}, []
    payload = zero

    def fetch(matrix, step):
        shifts = [step * merge + m for m in range(merge)]
        parts = after(payload, *[cut(held, matrix, lane(plane - shift)) for shift in shifts])
        return ("fetch", matrix, step, [rotate(part, -shift) for part, shift in zip(parts, shifts)])

    def deliver(matrix, step):
        shifts = [step * merge + m for m in range(merge)]
        parts = after(payload, *parts_of(outgoing[matrix, step]))
        return ("deliver", matrix, step, [rotate(part, shift) for part, shift in zip(parts, shifts)])

    def land(array, matrix, step, parts):
        for m, part in enumerate(parts):
            shift = step * merge + m
            array = lax.dynamic_update_slice(array, part[None, None], (matrix, lane(plane - shift), 0, 0))
        return array

    last_phase = groups - 2
    for turn in range(steps + 1):
        for phase in range(1, groups + 1):
            if turn == steps and phase > last_phase:
                break
            for matrix in range(2):
                tick = ((turn * groups) + phase - 1) * 2 + matrix
                landed = [entry for entry in transit if entry[0] <= tick]
                transit = [entry for entry in transit if entry[0] > tick]
                values = after(payload, from_left[matrix], from_right[matrix], *[p for e in landed for p in e[4]])
                here_left, here_right, values = values[0], values[1], list(values[2:])
                for _, kind, at, step, parts in landed:
                    parts, values = values[: len(parts)], values[len(parts) :]
                    if kind == "fetch":
                        moved[at, step] = join(parts)
                    else:
                        new_held = land(new_held, at, step, parts)
                if phase < groups:
                    to_right, to_left = here_left, here_right
                    if turn < steps:
                        right_owner = jnp.minimum(groups - phase + group, groups - 1)
                        left_owner = jnp.maximum(group - (groups - phase), 0)
                        to_right = jnp.where(group < phase, to_right + own(matrix, right_owner, order[turn]), to_right)
                        to_left = jnp.where(
                            groups - 1 - group < phase, to_left + own(matrix, left_owner, order[turn]), to_left
                        )
                else:
                    step = order[turn]
                    if (matrix, step) not in moved:
                        moved[matrix, step] = join(fetch(matrix, step)[3])
                    total = own(matrix, group, step) + here_left + here_right
                    mean_diff = total / groups
                    new_momentum = MOMENTUM_COEF * moved[matrix, step] + mean_diff
                    update = OUTER_RATE * (mean_diff + MOMENTUM_COEF * new_momentum)
                    outgoing[matrix, step] = new_momentum
                    if turn == steps - 1:
                        new_held = land(new_held, *deliver(matrix, step)[1:])
                    new_weights = write_weights(new_weights, matrix, group, step, update)
                    to_right = to_left = update
                payload = to_right
                from_left[matrix] = lax.ppermute(to_right, "grp", rightward)
                from_right[matrix] = lax.ppermute(to_left, "grp", leftward)
                place_in_turn = tick - turn * groups * 2
                if place_in_turn in (0, 2) and turn < steps - 1:
                    transit.append((tick + 2,) + fetch(place_in_turn // 2, order[turn]))
                if place_in_turn in (4, 6) and 0 < turn < steps:
                    transit.append((tick + 2,) + deliver(place_in_turn // 2 - 2, order[turn - 1]))
                if phase == groups:
                    arrived_left[matrix], arrived_right[matrix] = [], []
                arrived_left[matrix].append(from_left[matrix])
                arrived_right[matrix].append(from_right[matrix])
                if len(arrived_left[matrix]) == groups - 1 and turn > 0:
                    for hop in range(groups - 1):
                        update = jnp.where(
                            group > hop,
                            arrived_left[matrix][hop],
                            arrived_right[matrix][groups - 2 - hop],
                        )
                        owner = lax.rem(group + groups - 1 - hop, groups)
                        new_weights = write_weights(new_weights, matrix, owner, order[turn - 1], update)
    for _, _, at, step, parts in transit:
        new_held = land(new_held, at, step, parts)
    return (new_weights.reshape(start_weights.shape), new_held.reshape(momentum.shape))


def solution(mesh):
    in_specs = (
        P("grp", None, "shard", "tp"),
        P(None, "shard", "tp"),
        P(None, None, None, ("grp", "shard", "tp"), None, None),
    )
    out_specs = (P(None, "shard", "tp"), P(None, None, None, ("grp", "shard", "tp"), None, None))
    return jax.shard_map(body, mesh=mesh, in_specs=in_specs, out_specs=out_specs, check_vma=False)
```

```python
import jax
import jax.numpy as jnp
from jax import lax
from jax.experimental import pallas as pl
from jax.sharding import PartitionSpec as P

OUTER_RATE = 0.7
MOMENTUM_COEF = 0.5
STEPS = 8


def blank(shape):
    return pl.pallas_call(
        lambda out: None,
        out_shape=jax.ShapeDtypeStruct(shape, jnp.float32),
        out_specs=pl.BlockSpec(memory_space=pl.ANY),
    )()


def after(first, *arrays):
    return lax.optimization_barrier((first, *arrays))[1:]


def body(inner_weights, start_weights, momentum):
    groups = lax.axis_size("grp")
    plane = lax.axis_size("shard") * lax.axis_size("tp")
    place = lax.axis_index(("shard", "tp"))
    row_count, col_count = start_weights.shape[1:]
    q_rows = row_count // (groups * plane)
    steps = min(STEPS, plane)
    merge = plane // steps
    block = (q_rows, col_count)

    inner = inner_weights.reshape((2, groups, plane) + block)
    start = start_weights.reshape((2, groups, plane) + block)
    held = momentum.reshape((2, plane) + block)

    def rotate(part, shift):
        if shift % plane == 0:
            return part
        return lax.ppermute(part, ("shard", "tp"), [(i, (i + shift) % plane) for i in range(plane)])

    def shifts_of(step):
        return [step * merge + m for m in range(merge)]

    def join(parts, axis):
        return parts[0] if merge == 1 else jnp.concatenate(parts, axis=axis)

    def rows_of(array, step, place):
        return join([lax.dynamic_slice_in_dim(array, lax.rem(place + s, plane), 1, 2) for s in shifts_of(step)], 2)

    def fetch(step, place):
        parts = [lax.dynamic_slice_in_dim(held, lax.rem(place + plane - s, plane), 1, 1) for s in shifts_of(step)]
        return [rotate(part, -s) for part, s in zip(parts, shifts_of(step))]

    def deliver(step, value):
        return [rotate(value[:, m : m + 1], s) for m, s in enumerate(shifts_of(step))]

    def land(array, step, parts):
        for part, s in zip(parts, shifts_of(step)):
            array = lax.dynamic_update_slice_in_dim(array, part, lax.rem(place + plane - s, plane), 1)
        return array

    def spread(array, step, update):
        for m, s in enumerate(shifts_of(step)):
            at = (0, 0, lax.rem(place + s, plane), 0, 0)
            old = lax.dynamic_slice(start, at, (2, groups, 1) + block)
            array = lax.dynamic_update_slice(array, old - update[:, :, m : m + 1], at)
        return array

    new_weights = blank(start.shape)
    new_held = blank(held.shape)
    order = [(turn + 1) % steps for turn in range(steps)]
    now = place
    moved, sent, gathered = [fetch(order[0], place)], [], []
    for turn in range(steps):
        step = order[turn]
        total = lax.psum_scatter(
            rows_of(start, step, now) - rows_of(inner, step, now), "grp", scatter_dimension=1, tiled=True
        )[:, 0]
        if turn + 1 < steps:
            moved.append(fetch(order[turn + 1], now))
        mean_diff = total / groups
        new_momentum = MOMENTUM_COEF * join(moved[turn], 1) + mean_diff
        update = OUTER_RATE * (mean_diff + MOMENTUM_COEF * new_momentum)
        if turn == 0:
            (now,) = after(update, place)
        else:
            now, gathered[turn - 1], *sent[turn - 1] = after(update, place, gathered[turn - 1], *sent[turn - 1])
            new_held = land(new_held, order[turn - 1], sent[turn - 1])
            new_weights = spread(new_weights, order[turn - 1], gathered[turn - 1])
        sent.append(deliver(step, new_momentum))
        gathered.append(lax.all_gather(update[:, None], "grp", axis=1, tiled=True))
    new_held = land(new_held, order[-1], sent[-1])
    new_weights = spread(new_weights, order[-1], gathered[-1])
    return (new_weights.reshape(start_weights.shape), new_held.reshape(momentum.shape))


def solution(mesh):
    in_specs = (
        P("grp", None, "shard", "tp"),
        P(None, "shard", "tp"),
        P(None, None, None, ("grp", "shard", "tp"), None, None),
    )
    out_specs = (P(None, "shard", "tp"), P(None, None, None, ("grp", "shard", "tp"), None, None))
    return jax.shard_map(body, mesh=mesh, in_specs=in_specs, out_specs=out_specs, check_vma=False)
```

```python
import jax
import jax.numpy as jnp
from jax import lax
from jax.experimental import pallas as pl
from jax.sharding import PartitionSpec as P

OUTER_RATE = 0.7
MOMENTUM_COEF = 0.5
STEPS = 8


def blank(shape):
    return pl.pallas_call(
        lambda out: None,
        out_shape=jax.ShapeDtypeStruct(shape, jnp.float32),
        out_specs=pl.BlockSpec(memory_space=pl.ANY),
    )()


def after(first, *arrays):
    return lax.optimization_barrier((first, *arrays))[1:]


def body(inner_weights, start_weights, momentum):
    groups = lax.axis_size("grp")
    plane = lax.axis_size("shard") * lax.axis_size("tp")
    group = lax.axis_index("grp")
    place = lax.axis_index(("shard", "tp"))
    row_count, col_count = start_weights.shape[1:]
    q_rows = row_count // (groups * plane)
    steps = min(STEPS, plane)
    merge = plane // steps
    block = (q_rows, col_count)

    inner = inner_weights.reshape((2, groups, plane) + block)
    start = start_weights.reshape((2, groups, plane) + block)
    held = momentum.reshape((2, plane) + block)

    def rotate(part, shift):
        if shift % plane == 0:
            return part
        return lax.ppermute(part, ("shard", "tp"), [(i, (i + shift) % plane) for i in range(plane)])

    def shifts_of(step):
        return [step * merge + m for m in range(merge)]

    def join(parts, axis):
        return parts[0] if merge == 1 else jnp.concatenate(parts, axis=axis)

    def rows_of(array, step, place):
        return join([lax.dynamic_slice_in_dim(array, lax.rem(place + s, plane), 1, 2) for s in shifts_of(step)], 2)

    def fetch(step, place):
        parts = [lax.dynamic_slice_in_dim(held, lax.rem(place + plane - s, plane), 1, 1) for s in shifts_of(step)]
        return [rotate(part, -s) for part, s in zip(parts, shifts_of(step))]

    def deliver(step, value):
        return [rotate(value[:, m : m + 1], s) for m, s in enumerate(shifts_of(step))]

    def land(array, step, parts):
        for part, s in zip(parts, shifts_of(step)):
            array = lax.dynamic_update_slice_in_dim(array, part, lax.rem(place + plane - s, plane), 1)
        return array

    def spread(array, matrix, step, owner, update):
        for m, s in enumerate(shifts_of(step)):
            at = (matrix, owner, lax.rem(place + s, plane), 0, 0)
            old = lax.dynamic_slice(start, at, (1, 1, 1) + block)
            array = lax.dynamic_update_slice(array, old - update[m][None, None, None], at)
        return array

    def hop(number, to_right, to_left):
        right = [(i, i + 1) for i in range(number, groups - 1)]
        left = [(groups - 1 - i, groups - 2 - i) for i in range(number, groups - 1)]
        if 2 * number >= groups:
            came = lax.ppermute(jnp.where(group < groups - number, to_left, to_right), "grp", right + left)
            return came, came
        return lax.ppermute(to_right, "grp", right), lax.ppermute(to_left, "grp", left)

    def part_sum(step, place):
        differ = rows_of(start, step, place) - rows_of(inner, step, place)
        return lax.psum_scatter(differ, "grp", scatter_dimension=1, tiled=True)[:, 0]

    new_weights = blank(start.shape)
    new_held = blank(held.shape)
    order = [(turn + 1) % steps for turn in range(steps)]
    depth = min(3, steps)
    totals, now = [], place
    for step in order[:depth]:
        totals.append(part_sum(step, now))
    moved = fetch(order[0], place)
    sent = []
    for turn in range(steps):
        step = order[turn]
        mean_diff = totals[turn] / groups
        new_momentum = MOMENTUM_COEF * join(moved, 1) + mean_diff
        update = OUTER_RATE * (mean_diff + MOMENTUM_COEF * new_momentum)
        chains = [(update[matrix], update[matrix]) for matrix in range(2)]
        came = [[], []]
        for number in range(groups - 1):
            if number == 1:
                now, *sent = after(came[0][0][0], place, *sent)
                if sent:
                    new_held = land(new_held, order[turn - 1], sent)
                if turn + depth < steps:
                    totals.append(part_sum(order[turn + depth], now))
                if turn + 1 < steps:
                    moved = fetch(order[turn + 1], now)
            for matrix in range(2):
                to_right, to_left = chains[matrix]
                if number == groups - 2 and matrix == 0 and turn + 1 < steps:
                    to_right, to_left, *moved = lax.optimization_barrier((to_right, to_left, *moved))
                chains[matrix] = hop(number, to_right, to_left)
                came[matrix].append(chains[matrix])
        if turn + 1 < steps:
            last = came[1][groups - 3]
            (totals[turn + 1],) = after(last[0], totals[turn + 1])
            (new_momentum,) = after(last[1], new_momentum)
        sent = deliver(step, new_momentum)
        for matrix in range(2):
            new_weights = spread(new_weights, matrix, step, group, update[matrix])
            for number in range(groups - 1):
                from_left, from_right = came[matrix][number][0], came[matrix][groups - 2 - number][1]
                part = jnp.where(group > number, from_left, from_right)
                owner = lax.rem(group + groups - 1 - number, groups)
                new_weights = spread(new_weights, matrix, step, owner, part)
    new_held = land(new_held, order[-1], sent)
    return (new_weights.reshape(start_weights.shape), new_held.reshape(momentum.shape))


def solution(mesh):
    in_specs = (
        P("grp", None, "shard", "tp"),
        P(None, "shard", "tp"),
        P(None, None, None, ("grp", "shard", "tp"), None, None),
    )
    out_specs = (P(None, "shard", "tp"), P(None, None, None, ("grp", "shard", "tp"), None, None))
    return jax.shard_map(body, mesh=mesh, in_specs=in_specs, out_specs=out_specs, check_vma=False)
```

```python
import jax
import jax.numpy as jnp
from jax import lax
from jax.experimental import pallas as pl
from jax.sharding import PartitionSpec as P

OUTER_RATE = 0.7
MOMENTUM_COEF = 0.5
STEPS = 8
STREAMS = 2


def blank(shape):
    return pl.pallas_call(
        lambda out: None,
        out_shape=jax.ShapeDtypeStruct(shape, jnp.float32),
        out_specs=pl.BlockSpec(memory_space=pl.ANY),
    )()


def body(inner_weights, start_weights, momentum):
    groups = lax.axis_size("grp")
    shards = lax.axis_size("shard")
    tp_size = lax.axis_size("tp")
    plane = shards * tp_size
    group = lax.axis_index("grp")
    place = lax.axis_index(("shard", "tp"))
    row_count, col_count = start_weights.shape[1:]
    q_rows = row_count // (groups * plane)
    steps = min(STEPS, plane)
    merge = plane // steps
    turns = steps // STREAMS
    block = (q_rows, col_count)

    inner = inner_weights.reshape((2, groups, plane) + block)
    start = start_weights.reshape((2, groups, plane) + block)
    held = momentum.reshape((2, plane) + block)
    rightward = [(i, i + 1) for i in range(groups - 1)]
    leftward = [(i + 1, i) for i in range(groups - 1)]

    def lane(shift):
        return lax.rem(place + shift, plane)

    def shifts_of(step):
        return [step * merge + m for m in range(merge)]

    def join(parts):
        return parts[0] if merge == 1 else jnp.concatenate(parts, axis=1)

    def parts_of(chunk):
        return [chunk[:, m * q_rows : (m + 1) * q_rows] for m in range(merge)]

    def rows_of(array, owner, step):
        def cut(shift):
            return lax.dynamic_slice(array, (0, owner, lane(shift), 0, 0), (2, 1, 1) + block).reshape((2,) + block)

        return join([cut(shift) for shift in shifts_of(step)])

    def own(owner, step):
        return rows_of(start, owner, step) - rows_of(inner, owner, step)

    def rotate(part, shift):
        if shift % plane == 0:
            return part
        return lax.ppermute(part, ("shard", "tp"), [(i, (i + shift) % plane) for i in range(plane)])

    new_weights = blank(start.shape)
    new_held = blank(held.shape)

    def write_weights(array, owner, step, update):
        for shift, part in zip(shifts_of(step), parts_of(update)):
            at = (0, owner, lane(shift), 0, 0)
            old = lax.dynamic_slice(start, at, (2, 1, 1) + block)
            array = lax.dynamic_update_slice(array, old - part[:, None, None], at)
        return array

    def after(first, *arrays):
        return lax.optimization_barrier((first, *arrays))[1:]

    order = [[(stream * turns + turn + 1) % steps for turn in range(turns)] for stream in range(STREAMS)]
    zero = jnp.zeros((2, merge * q_rows, col_count), jnp.float32)
    from_left, from_right = [zero] * STREAMS, [zero] * STREAMS
    arrived_left, arrived_right = [[]] * STREAMS, [[]] * STREAMS
    moved, outgoing, transit = {}, {}, []
    payload = zero

    def fetch(step):
        parts = [lax.dynamic_slice_in_dim(held, lane(plane - shift), 1, 1)[:, 0] for shift in shifts_of(step)]
        parts = after(payload, *parts)
        return ("fetch", step, [rotate(part, -shift) for part, shift in zip(parts, shifts_of(step))])

    def deliver(step):
        parts = after(payload, *parts_of(outgoing[step]))
        return ("deliver", step, [rotate(part, shift) for part, shift in zip(parts, shifts_of(step))])

    def land(array, step, parts):
        for shift, part in zip(shifts_of(step), parts):
            array = lax.dynamic_update_slice_in_dim(array, part[:, None], lane(plane - shift), 1)
        return array

    for turn in range(turns + 1):
        for phase in range(1, groups + 1):
            if turn == turns and phase > groups - 2:
                break
            for stream in range(STREAMS):
                in_turn = (phase - 1) * STREAMS + stream
                tick = turn * groups * STREAMS + in_turn
                landed = [entry for entry in transit if entry[0] <= tick]
                transit = [entry for entry in transit if entry[0] > tick]
                values = after(payload, from_left[stream], from_right[stream], *[p for e in landed for p in e[3]])
                here_left, here_right, values = values[0], values[1], list(values[2:])
                for _, kind, step, parts in landed:
                    parts, values = values[: len(parts)], values[len(parts) :]
                    if kind == "fetch":
                        moved[step] = join(parts)
                    else:
                        new_held = land(new_held, step, parts)
                step = order[stream][turn] if turn < turns else None
                if phase < groups:
                    to_right, to_left = here_left, here_right
                    if turn < turns:
                        right_owner = jnp.minimum(groups - phase + group, groups - 1)
                        left_owner = jnp.maximum(group - (groups - phase), 0)
                        to_right = jnp.where(group < phase, to_right + own(right_owner, step), to_right)
                        to_left = jnp.where(groups - 1 - group < phase, to_left + own(left_owner, step), to_left)
                else:
                    if step not in moved:
                        moved[step] = join(fetch(step)[2])
                    total = own(group, step) + here_left + here_right
                    mean_diff = total / groups
                    new_momentum = MOMENTUM_COEF * moved[step] + mean_diff
                    update = OUTER_RATE * (mean_diff + MOMENTUM_COEF * new_momentum)
                    outgoing[step] = new_momentum
                    if step == 0:
                        new_held = land(new_held, *deliver(step)[1:])
                    new_weights = write_weights(new_weights, group, step, update)
                    to_right = to_left = update
                payload = to_right
                from_left[stream] = lax.ppermute(to_right, "grp", rightward)
                from_right[stream] = lax.ppermute(to_left, "grp", leftward)
                slot = in_turn // 2
                if in_turn % 2 == 0 and slot < STREAMS and turn < turns and order[slot][turn] != 0:
                    transit.append((tick + 2,) + fetch(order[slot][turn]))
                slot = slot - STREAMS if turn < turns else slot
                if in_turn % 2 == 0 and 0 <= slot < STREAMS and turn > 0 and order[slot][turn - 1] != 0:
                    transit.append((tick + 2,) + deliver(order[slot][turn - 1]))
                if phase == groups:
                    arrived_left[stream], arrived_right[stream] = [], []
                arrived_left[stream].append(from_left[stream])
                arrived_right[stream].append(from_right[stream])
                if len(arrived_left[stream]) == groups - 1 and turn > 0:
                    for hop in range(groups - 1):
                        update = jnp.where(
                            group > hop,
                            arrived_left[stream][hop],
                            arrived_right[stream][groups - 2 - hop],
                        )
                        owner = lax.rem(group + groups - 1 - hop, groups)
                        new_weights = write_weights(new_weights, owner, order[stream][turn - 1], update)
    for _, _, step, parts in transit:
        new_held = land(new_held, step, parts)
    return (new_weights.reshape(start_weights.shape), new_held.reshape(momentum.shape))


def solution(mesh):
    in_specs = (
        P("grp", None, "shard", "tp"),
        P(None, "shard", "tp"),
        P(None, None, None, ("grp", "shard", "tp"), None, None),
    )
    out_specs = (P(None, "shard", "tp"), P(None, None, None, ("grp", "shard", "tp"), None, None))
    return jax.shard_map(body, mesh=mesh, in_specs=in_specs, out_specs=out_specs, check_vma=False)
```

```python
import jax
import jax.numpy as jnp
from jax import lax
from jax.experimental import pallas as pl
from jax.sharding import PartitionSpec as P

OUTER_RATE = 0.7
MOMENTUM_COEF = 0.5
STEPS = 8
STREAMS = 2


def blank(shape):
    return pl.pallas_call(
        lambda out: None,
        out_shape=jax.ShapeDtypeStruct(shape, jnp.float32),
        out_specs=pl.BlockSpec(memory_space=pl.ANY),
    )()


def body(inner_weights, start_weights, momentum):
    groups = lax.axis_size("grp")
    shards = lax.axis_size("shard")
    tp_size = lax.axis_size("tp")
    plane = shards * tp_size
    group = lax.axis_index("grp")
    place = lax.axis_index(("shard", "tp"))
    row_count, col_count = start_weights.shape[1:]
    q_rows = row_count // (groups * plane)
    steps = min(STEPS, plane)
    merge = plane // steps
    turns = steps // STREAMS
    block = (q_rows, col_count)

    inner = inner_weights.reshape((2, groups, plane) + block)
    start = start_weights.reshape((2, groups, plane) + block)
    held = momentum.reshape((2, plane) + block)
    rightward = [(i, i + 1) for i in range(groups - 1)]
    leftward = [(i + 1, i) for i in range(groups - 1)]

    def lane(shift):
        return lax.rem(place + shift, plane)

    def shifts_of(step):
        return [step * merge + m for m in range(merge)]

    def join(parts):
        return parts[0] if merge == 1 else jnp.concatenate(parts, axis=1)

    def parts_of(chunk):
        return [chunk[:, m * q_rows : (m + 1) * q_rows] for m in range(merge)]

    def rows_of(array, owner, step):
        def cut(shift):
            return lax.dynamic_slice(array, (0, owner, lane(shift), 0, 0), (2, 1, 1) + block).reshape((2,) + block)

        return join([cut(shift) for shift in shifts_of(step)])

    def own(owner, step):
        return rows_of(start, owner, step) - rows_of(inner, owner, step)

    def rotate(part, shift):
        if shift % plane == 0:
            return part
        return lax.ppermute(part, ("shard", "tp"), [(i, (i + shift) % plane) for i in range(plane)])

    new_weights = blank(start.shape)
    new_held = blank(held.shape)

    def write_weights(array, owner, step, update):
        for shift, part in zip(shifts_of(step), parts_of(update)):
            at = (0, owner, lane(shift), 0, 0)
            old = lax.dynamic_slice(start, at, (2, 1, 1) + block)
            array = lax.dynamic_update_slice(array, old - part[:, None, None], at)
        return array

    def after(first, *arrays):
        return lax.optimization_barrier((*first, *arrays))[len(first) :]

    order = [[(stream * turns + turn + 1) % steps for turn in range(turns)] for stream in range(STREAMS)]
    zero = jnp.zeros((2, merge * q_rows, col_count), jnp.float32)
    from_left, from_right = [zero] * STREAMS, [zero] * STREAMS
    arrived_left, arrived_right = [[]] * STREAMS, [[]] * STREAMS
    moved, outgoing, transit = {}, {}, []
    payload = (zero,)

    def fetch(step):
        (here,) = after(payload, place)
        parts = []
        for shift in shifts_of(step):
            at = lax.rem(here + plane - shift, plane)
            halves = [lax.dynamic_slice(held, (matrix, at, 0, 0), (1, 1) + block)[0] for matrix in range(2)]
            parts.append(jnp.concatenate(halves, axis=0))
        return ("fetch", step, [rotate(part, -shift) for part, shift in zip(parts, shifts_of(step))])

    def deliver(step):
        parts = after(payload, *parts_of(outgoing[step]))
        return ("deliver", step, [rotate(part, shift) for part, shift in zip(parts, shifts_of(step))])

    def land(array, step, parts):
        for shift, part in zip(shifts_of(step), parts):
            array = lax.dynamic_update_slice_in_dim(array, part[:, None], lane(plane - shift), 1)
        return array

    for turn in range(turns + 1):
        for phase in range(1, groups + 1):
            if turn == turns and phase > groups - 2:
                break
            for stream in range(STREAMS):
                in_turn = (phase - 1) * STREAMS + stream
                tick = turn * groups * STREAMS + in_turn
                landed = [entry for entry in transit if entry[0] <= tick]
                transit = [entry for entry in transit if entry[0] > tick]
                values = after(payload, from_left[stream], from_right[stream], *[p for e in landed for p in e[3]])
                here_left, here_right, values = values[0], values[1], list(values[2:])
                for _, kind, step, parts in landed:
                    parts, values = values[: len(parts)], values[len(parts) :]
                    if kind == "fetch":
                        moved[step] = join(parts)
                    else:
                        new_held = land(new_held, step, parts)
                step = order[stream][turn] if turn < turns else None
                if phase < groups:
                    to_right, to_left = here_left, here_right
                    if turn < turns:
                        right_owner = jnp.minimum(groups - phase + group, groups - 1)
                        left_owner = jnp.maximum(group - (groups - phase), 0)
                        to_right = jnp.where(group < phase, to_right + own(right_owner, step), to_right)
                        to_left = jnp.where(groups - 1 - group < phase, to_left + own(left_owner, step), to_left)
                else:
                    if step not in moved:
                        moved[step] = join(fetch(step)[2])
                    total = own(group, step) + here_left + here_right
                    mean_diff = total / groups
                    new_momentum = MOMENTUM_COEF * moved[step] + mean_diff
                    update = OUTER_RATE * (mean_diff + MOMENTUM_COEF * new_momentum)
                    outgoing[step] = new_momentum
                    if step == 0:
                        new_held = land(new_held, *deliver(step)[1:])
                    new_weights = write_weights(new_weights, group, step, update)
                    to_right = to_left = update
                payload = (to_right, to_left)
                from_left[stream] = lax.ppermute(to_right, "grp", rightward)
                from_right[stream] = lax.ppermute(to_left, "grp", leftward)
                slot = in_turn // 2
                if in_turn % 2 == 0 and slot < STREAMS and turn < turns and order[slot][turn] != 0:
                    transit.append((tick + 2,) + fetch(order[slot][turn]))
                slot = slot - STREAMS if turn < turns else slot
                if in_turn % 2 == 0 and 0 <= slot < STREAMS and turn > 0 and order[slot][turn - 1] != 0:
                    transit.append((tick + 2,) + deliver(order[slot][turn - 1]))
                if phase == groups:
                    arrived_left[stream], arrived_right[stream] = [], []
                arrived_left[stream].append(from_left[stream])
                arrived_right[stream].append(from_right[stream])
                if len(arrived_left[stream]) == groups - 1 and turn > 0:
                    for hop in range(groups - 1):
                        update = jnp.where(
                            group > hop,
                            arrived_left[stream][hop],
                            arrived_right[stream][groups - 2 - hop],
                        )
                        owner = lax.rem(group + groups - 1 - hop, groups)
                        new_weights = write_weights(new_weights, owner, order[stream][turn - 1], update)
    for _, _, step, parts in transit:
        new_held = land(new_held, step, parts)
    return (new_weights.reshape(start_weights.shape), new_held.reshape(momentum.shape))


def solution(mesh):
    in_specs = (
        P("grp", None, "shard", "tp"),
        P(None, "shard", "tp"),
        P(None, None, None, ("grp", "shard", "tp"), None, None),
    )
    out_specs = (P(None, "shard", "tp"), P(None, None, None, ("grp", "shard", "tp"), None, None))
    return jax.shard_map(body, mesh=mesh, in_specs=in_specs, out_specs=out_specs, check_vma=False)
```

```python
import jax
import jax.numpy as jnp
from jax import lax
from jax.experimental import pallas as pl
from jax.sharding import PartitionSpec as P

OUTER_RATE = 0.7
MOMENTUM_COEF = 0.5
STEPS = 8


def blank(shape):
    return pl.pallas_call(
        lambda out: None,
        out_shape=jax.ShapeDtypeStruct(shape, jnp.float32),
        out_specs=pl.BlockSpec(memory_space=pl.ANY),
    )()


def body(inner_weights, start_weights, momentum):
    groups = lax.axis_size("grp")
    shards = lax.axis_size("shard")
    tp_size = lax.axis_size("tp")
    plane = shards * tp_size
    group = lax.axis_index("grp")
    place = lax.axis_index(("shard", "tp"))
    row_count, col_count = start_weights.shape[1:]
    q_rows = row_count // (groups * plane)
    steps = min(STEPS, plane)
    merge = plane // steps
    block = (q_rows, col_count)

    inner = inner_weights.reshape((2, groups, plane) + block)
    start = start_weights.reshape((2, groups, plane) + block)
    held = momentum.reshape((2, plane) + block)
    rightward = [(i, i + 1) for i in range(groups - 1)]
    leftward = [(i + 1, i) for i in range(groups - 1)]

    def lane(shift):
        return lax.rem(place + shift, plane)

    def shifts_of(step):
        return [step * merge + m for m in range(merge)]

    def join(parts):
        return parts[0] if len(parts) == 1 else jnp.concatenate(parts, axis=0)

    def rows_of(array, matrix, owner, step):
        def cut(shift):
            return lax.dynamic_slice(array, (matrix, owner, lane(shift), 0, 0), (1, 1, 1) + block).reshape(block)

        return join([cut(shift) for shift in shifts_of(step)])

    def own(matrix, owner, step):
        return rows_of(start, matrix, owner, step) - rows_of(inner, matrix, owner, step)

    def rotate(part, shift):
        if shift % plane == 0:
            return part
        return lax.ppermute(part, ("shard", "tp"), [(i, (i + shift) % plane) for i in range(plane)])

    new_weights = blank(start.shape)
    new_held = blank(held.shape)

    def write_weights(array, matrix, owner, step, update):
        for m, shift in enumerate(shifts_of(step)):
            at = (matrix, owner, lane(shift), 0, 0)
            old = lax.dynamic_slice(start, at, (1, 1, 1) + block)
            part = update[m * q_rows : (m + 1) * q_rows]
            array = lax.dynamic_update_slice(array, old - part[None, None, None], at)
        return array

    def after(first, *arrays):
        return lax.optimization_barrier((*first, *arrays))[len(first) :]

    order = [(turn + 1) % steps for turn in range(steps)]
    zero = jnp.zeros((merge * q_rows, col_count), jnp.float32)
    from_left, from_right = [zero, zero], [zero, zero]
    arrived_left, arrived_right = [[], []], [[], []]
    moved, outgoing, transit = {}, {}, []
    payload = (zero,)

    def fetch(step):
        (here,) = after(payload, place)
        parts = []
        for shift in shifts_of(step):
            at = lax.rem(here + plane - shift, plane)
            halves = [lax.dynamic_slice(held, (matrix, at, 0, 0), (1, 1) + block)[0] for matrix in range(2)]
            parts.append(jnp.stack([half[0] for half in halves]))
        return ("fetch", step, [rotate(part, -shift) for part, shift in zip(parts, shifts_of(step))])

    def deliver(step):
        halves = after(payload, *outgoing[step])
        parts = []
        for m, shift in enumerate(shifts_of(step)):
            parts.append(jnp.stack([half[m * q_rows : (m + 1) * q_rows] for half in halves]))
        return ("deliver", step, [rotate(part, shift) for part, shift in zip(parts, shifts_of(step))])

    def land(array, step, parts):
        for shift, part in zip(shifts_of(step), parts):
            array = lax.dynamic_update_slice(array, part[:, None], (0, lane(plane - shift), 0, 0))
        return array

    for turn in range(steps + 1):
        for phase in range(1, groups + 1):
            if turn == steps and phase > groups - 2:
                break
            for matrix in range(2):
                in_turn = (phase - 1) * 2 + matrix
                tick = turn * groups * 2 + in_turn
                landed = [entry for entry in transit if entry[0] <= tick]
                transit = [entry for entry in transit if entry[0] > tick]
                values = after(payload, from_left[matrix], from_right[matrix], *[p for e in landed for p in e[3]])
                here_left, here_right, values = values[0], values[1], list(values[2:])
                for _, kind, step, parts in landed:
                    parts, values = values[: len(parts)], values[len(parts) :]
                    if kind == "fetch":
                        moved[step] = parts
                    else:
                        new_held = land(new_held, step, parts)
                step = order[turn] if turn < steps else None
                if phase < groups:
                    to_right, to_left = here_left, here_right
                    if turn < steps:
                        right_owner = jnp.minimum(groups - phase + group, groups - 1)
                        left_owner = jnp.maximum(group - (groups - phase), 0)
                        to_right = jnp.where(group < phase, to_right + own(matrix, right_owner, step), to_right)
                        to_left = jnp.where(groups - 1 - group < phase, to_left + own(matrix, left_owner, step), to_left)
                else:
                    total = own(matrix, group, step) + here_left + here_right
                    mean_diff = total / groups
                    old_momentum = join([part[matrix] for part in moved[step]])
                    new_momentum = MOMENTUM_COEF * old_momentum + mean_diff
                    update = OUTER_RATE * (mean_diff + MOMENTUM_COEF * new_momentum)
                    outgoing.setdefault(step, []).append(new_momentum)
                    new_weights = write_weights(new_weights, matrix, group, step, update)
                    to_right = to_left = update
                payload = (to_right, to_left)
                from_left[matrix] = lax.ppermute(to_right, "grp", rightward)
                from_right[matrix] = lax.ppermute(to_left, "grp", leftward)
                if in_turn == 0 and turn < steps:
                    transit.append((tick + groups,) + fetch(order[turn]))
                if in_turn == groups and 0 < turn < steps:
                    transit.append((tick + groups,) + deliver(order[turn - 1]))
                if phase == groups:
                    arrived_left[matrix], arrived_right[matrix] = [], []
                arrived_left[matrix].append(from_left[matrix])
                arrived_right[matrix].append(from_right[matrix])
                if len(arrived_left[matrix]) == groups - 1 and turn > 0:
                    for hop in range(groups - 1):
                        update = jnp.where(
                            group > hop,
                            arrived_left[matrix][hop],
                            arrived_right[matrix][groups - 2 - hop],
                        )
                        owner = lax.rem(group + groups - 1 - hop, groups)
                        new_weights = write_weights(new_weights, matrix, owner, order[turn - 1], update)
    new_held = land(new_held, *deliver(order[-1])[1:])
    return (new_weights.reshape(start_weights.shape), new_held.reshape(momentum.shape))


def solution(mesh):
    in_specs = (
        P("grp", None, "shard", "tp"),
        P(None, "shard", "tp"),
        P(None, None, None, ("grp", "shard", "tp"), None, None),
    )
    out_specs = (P(None, "shard", "tp"), P(None, None, None, ("grp", "shard", "tp"), None, None))
    return jax.shard_map(body, mesh=mesh, in_specs=in_specs, out_specs=out_specs, check_vma=False)
```

```python
import jax
import jax.numpy as jnp
from jax import lax
from jax.experimental import pallas as pl
from jax.sharding import PartitionSpec as P

OUTER_RATE = 0.7
MOMENTUM_COEF = 0.5
BLOCKS = 4
CUTS = 3
ORDER = ((1, 3), (2, 0))


def blank(shape):
    return pl.pallas_call(
        lambda out: None,
        out_shape=jax.ShapeDtypeStruct(shape, jnp.float32),
        out_specs=pl.BlockSpec(memory_space=pl.ANY),
    )()


def mix(adds, term, passed):
    width = max(term.shape[2], passed.shape[2])
    term, passed = [jnp.pad(array, ((0, 0), (0, 0), (0, width - array.shape[2]))) for array in (term, passed)]
    return jnp.where(adds, passed + term, passed)


def body(inner_weights, start_weights, momentum):
    groups = lax.axis_size("grp")
    plane = lax.axis_size("shard") * lax.axis_size("tp")
    group = lax.axis_index("grp")
    place = lax.axis_index(("shard", "tp"))
    row_count, col_count = start_weights.shape[1:]
    lanes = plane // BLOCKS
    q_rows = row_count // (groups * plane)
    rows = lanes * q_rows
    streams = len(ORDER)

    inner = inner_weights.reshape(2, groups, BLOCKS, rows, col_count)
    start = start_weights.reshape(2, groups, BLOCKS, rows, col_count)
    held = momentum.reshape(2, plane, q_rows, col_count)
    rightward = [(i, i + 1) for i in range(groups - 1)]
    leftward = [(i + 1, i) for i in range(groups - 1)]

    wide = -(-col_count // (128 * CUTS)) * 128
    narrow = col_count - (CUTS - 1) * wide
    parts = []
    for blocks in ORDER:
        widths = [narrow] + [wide] * (2 * CUTS - 2) + [narrow]
        firsts = [sum(widths[at - at % CUTS : at]) for at in range(2 * CUTS)]
        parts.append([(blocks[at // CUTS], firsts[at], widths[at]) for at in range(2 * CUTS)])
    turns = 2 * CUTS

    def spot(block):
        return lax.bitwise_xor(place // lanes, block)

    def rows_of(array, owner, part):
        block, first, width = part
        return lax.dynamic_slice(array, (0, owner, spot(block), 0, first), (2, 1, 1, rows, width))[:, 0, 0]

    def own(owner, part):
        return rows_of(start, owner, part) - rows_of(inner, owner, part)

    def write_weights(array, owner, part, update):
        block, first, _ = part
        value = rows_of(start, owner, part) - update
        return lax.dynamic_update_slice(array, value[:, None, None], (0, owner, spot(block), 0, first))

    def after(first, *arrays):
        return lax.optimization_barrier((*first, *arrays))[len(first) :]

    def swap(array, key):
        (here,) = after(payload, place)
        at = lax.bitwise_xor(here, key)
        lane = jnp.stack([lax.dynamic_slice(array, (m, at, 0, 0), (1, 1, q_rows, col_count))[0, 0] for m in range(2)])
        if key == 0:
            return lane
        return lax.ppermute(lane, ("shard", "tp"), [(i, i ^ key) for i in range(plane)])

    def land(array, key, lane):
        return lax.dynamic_update_slice(array, lane[:, None], (0, lax.bitwise_xor(place, key), 0, 0))

    plan = {}
    ticks = (turns * groups + groups - 2) * streams
    for half in range(2):
        keys = [ORDER[stream][half] * lanes + r for stream in range(streams) for r in reversed(range(lanes))]
        for at, key in enumerate(keys):
            need = (half * CUTS + 1) * groups * streams - streams + at // lanes
            ready = ((half + 1) * CUTS * groups - 1) * streams
            if half == 0:
                fetch = min(4 * at // lanes, need - 1)
                deliver = ready + 2 + 8 * at // lanes
            else:
                fetch = groups * streams + 8 * at // lanes
                deliver = min(ready + 4 * at // lanes, ticks - 1)
            plan.setdefault(fetch, []).append(("fetch", key, min(fetch + 2 + half, need)))
            plan.setdefault(deliver, []).append(("deliver", key, deliver + 3 - half))

    new_weights = blank(start.shape)
    new_held = blank(held.shape)
    old, new = blank(held.shape), blank(held.shape)
    payload = (place,)
    zero = jnp.zeros((2, rows, narrow), jnp.float32)
    from_left, from_right = [zero] * streams, [zero] * streams
    arrived_left, arrived_right = [[] for _ in ORDER], [[] for _ in ORDER]
    transit = []

    for tick in range(ticks):
        turn, phase, stream = tick // (groups * streams), tick // streams % groups + 1, tick % streams
        landed = [entry for entry in transit if entry[2] <= tick]
        transit = [entry for entry in transit if entry[2] > tick]
        values = after(payload, from_left[stream], from_right[stream], *[entry[3] for entry in landed])
        here_left, here_right = values[:2]
        for (kind, key, _, _), lane in zip(landed, values[2:]):
            if kind == "fetch":
                old = land(old, key, lane)
            else:
                new_held = land(new_held, key, lane)
        part = parts[stream][turn] if turn < turns else None
        if phase < groups:
            to_right, to_left = here_left, here_right
            if turn < turns:
                right_owner = jnp.minimum(groups - phase + group, groups - 1)
                left_owner = jnp.maximum(group - (groups - phase), 0)
                to_right = mix(group < phase, own(right_owner, part), to_right)
                to_left = mix(groups - 1 - group < phase, own(left_owner, part), to_left)
        else:
            block, first, width = part
            total = own(group, part) + here_left[:, :, :width] + here_right[:, :, :width]
            mean_diff = total / groups
            mine = old.reshape(2, BLOCKS, rows, col_count)
            old_momentum = lax.dynamic_slice(mine, (0, spot(block), 0, first), (2, 1, rows, width))[:, 0]
            new_momentum = MOMENTUM_COEF * old_momentum + mean_diff
            update = OUTER_RATE * (mean_diff + MOMENTUM_COEF * new_momentum)
            mine = new.reshape(2, BLOCKS, rows, col_count)
            mine = lax.dynamic_update_slice(mine, new_momentum[:, None], (0, spot(block), 0, first))
            new = mine.reshape(held.shape)
            new_weights = write_weights(new_weights, group, part, update)
            to_right = to_left = update
        payload = (to_right, to_left)
        from_left[stream] = lax.ppermute(to_right, "grp", rightward)
        from_right[stream] = lax.ppermute(to_left, "grp", leftward)
        for kind, key, use in plan.get(tick, []):
            transit.append((kind, key, use, swap(held if kind == "fetch" else new, key)))
        if phase == groups:
            arrived_left[stream], arrived_right[stream] = [], []
        arrived_left[stream].append(from_left[stream])
        arrived_right[stream].append(from_right[stream])
        if len(arrived_left[stream]) == groups - 1 and turn > 0:
            part = parts[stream][turn - 1]
            width = part[2]
            for hop in range(groups - 1):
                update = jnp.where(
                    group > hop,
                    arrived_left[stream][hop][:, :, :width],
                    arrived_right[stream][groups - 2 - hop][:, :, :width],
                )
                owner = lax.rem(group + groups - 1 - hop, groups)
                new_weights = write_weights(new_weights, owner, part, update)
    for _, key, _, lane in transit:
        new_held = land(new_held, key, lane)
    return (new_weights.reshape(start_weights.shape), new_held.reshape(momentum.shape))


def solution(mesh):
    in_specs = (
        P("grp", None, "shard", "tp"),
        P(None, "shard", "tp"),
        P(None, None, None, ("grp", "shard", "tp"), None, None),
    )
    out_specs = (P(None, "shard", "tp"), P(None, None, None, ("grp", "shard", "tp"), None, None))
    return jax.shard_map(body, mesh=mesh, in_specs=in_specs, out_specs=out_specs, check_vma=False)
```

```python
import jax
import jax.numpy as jnp
from jax import lax
from jax.experimental import pallas as pl
from jax.sharding import PartitionSpec as P

OUTER_RATE = 0.7
MOMENTUM_COEF = 0.5
STEPS = 8
STREAMS = 2


def blank(shape):
    return pl.pallas_call(
        lambda out: None,
        out_shape=jax.ShapeDtypeStruct(shape, jnp.float32),
        out_specs=pl.BlockSpec(memory_space=pl.ANY),
    )()


def body(inner_weights, start_weights, momentum):
    groups = lax.axis_size("grp")
    shards = lax.axis_size("shard")
    tp_size = lax.axis_size("tp")
    plane = shards * tp_size
    group = lax.axis_index("grp")
    place = lax.axis_index(("shard", "tp"))
    row_count, col_count = start_weights.shape[1:]
    q_rows = row_count // (groups * plane)
    steps = min(STEPS, plane)
    merge = plane // steps
    turns = steps // STREAMS
    block = (q_rows, col_count)

    inner = inner_weights.reshape((2, groups, plane) + block)
    start = start_weights.reshape((2, groups, plane) + block)
    held = momentum.reshape((2, plane) + block)
    rightward = [(i, i + 1) for i in range(groups - 1)]
    leftward = [(i + 1, i) for i in range(groups - 1)]

    def lane(shift):
        return lax.rem(place + shift, plane)

    def shifts_of(step):
        return [step * merge + m for m in range(merge)]

    def join(parts):
        return parts[0] if merge == 1 else jnp.concatenate(parts, axis=1)

    def parts_of(chunk):
        return [chunk[:, m * q_rows : (m + 1) * q_rows] for m in range(merge)]

    def rows_of(array, owner, step):
        def cut(shift):
            return lax.dynamic_slice(array, (0, owner, lane(shift), 0, 0), (2, 1, 1) + block).reshape((2,) + block)

        return join([cut(shift) for shift in shifts_of(step)])

    def own(owner, step):
        return rows_of(start, owner, step) - rows_of(inner, owner, step)

    def rotate(part, shift):
        if shift % plane == 0:
            return part
        return lax.ppermute(part, ("shard", "tp"), [(i, (i + shift) % plane) for i in range(plane)])

    new_weights = blank(start.shape)
    new_held = blank(held.shape)

    def write_weights(array, owner, step, value):
        for shift, part in zip(shifts_of(step), parts_of(value)):
            array = lax.dynamic_update_slice(array, part[:, None, None], (0, owner, lane(shift), 0, 0))
        return array

    def after(first, *arrays):
        return lax.optimization_barrier((*first, *arrays))[len(first) :]

    order = [[(stream * turns + turn + 1) % steps for turn in range(turns)] for stream in range(STREAMS)]
    zero = jnp.zeros((2, merge * q_rows, col_count), jnp.float32)
    from_left, from_right = [zero] * STREAMS, [zero] * STREAMS
    arrived_left, arrived_right = [[]] * STREAMS, [[]] * STREAMS
    moved, outgoing, transit = {}, {}, []
    payload = (zero,)

    def fetch(step):
        (here,) = after(payload, place)
        parts = []
        for shift in shifts_of(step):
            at = lax.rem(here + plane - shift, plane)
            halves = [lax.dynamic_slice(held, (matrix, at, 0, 0), (1, 1) + block)[0] for matrix in range(2)]
            parts.append(jnp.concatenate(halves, axis=0))
        return ("fetch", step, [rotate(part, -shift) for part, shift in zip(parts, shifts_of(step))])

    def deliver(step):
        parts = after(payload, *parts_of(outgoing[step]))
        return ("deliver", step, [rotate(part, shift) for part, shift in zip(parts, shifts_of(step))])

    def land(array, step, parts):
        for shift, part in zip(shifts_of(step), parts):
            array = lax.dynamic_update_slice_in_dim(array, part[:, None], lane(plane - shift), 1)
        return array

    for turn in range(turns + 1):
        for phase in range(1, groups + 1):
            if turn == turns and phase > groups - 2:
                break
            for stream in range(STREAMS):
                in_turn = (phase - 1) * STREAMS + stream
                tick = turn * groups * STREAMS + in_turn
                landed = [entry for entry in transit if entry[0] <= tick]
                transit = [entry for entry in transit if entry[0] > tick]
                values = after(payload, from_left[stream], from_right[stream], *[p for e in landed for p in e[3]])
                here_left, here_right, values = values[0], values[1], list(values[2:])
                for _, kind, step, parts in landed:
                    parts, values = values[: len(parts)], values[len(parts) :]
                    if kind == "fetch":
                        moved[step] = join(parts)
                    else:
                        new_held = land(new_held, step, parts)
                step = order[stream][turn] if turn < turns else None
                alone = None
                if turn == 0 and phase == 1:
                    (owner,) = after(payload, jnp.where(group == 0, groups - 1, 0))
                    alone = own(owner, step)
                    to_right = to_left = alone
                elif turn == turns and phase == groups - 2:
                    alone = jnp.where(group >= groups // 2, here_left, here_right)
                    to_right = to_left = alone
                elif phase < groups:
                    to_right, to_left = here_left, here_right
                    if turn < turns:
                        right_owner = jnp.minimum(groups - phase + group, groups - 1)
                        left_owner = jnp.maximum(group - (groups - phase), 0)
                        to_right = jnp.where(group < phase, to_right + own(right_owner, step), to_right)
                        to_left = jnp.where(groups - 1 - group < phase, to_left + own(left_owner, step), to_left)
                else:
                    if step not in moved:
                        moved[step] = join(fetch(step)[2])
                    total = own(group, step) + here_left + here_right
                    mean_diff = total / groups
                    new_momentum = MOMENTUM_COEF * moved[step] + mean_diff
                    update = OUTER_RATE * (mean_diff + MOMENTUM_COEF * new_momentum)
                    outgoing[step] = new_momentum
                    if step == 0:
                        new_held = land(new_held, *deliver(step)[1:])
                    fresh = rows_of(start, group, step) - update
                    new_weights = write_weights(new_weights, group, step, fresh)
                    to_right = to_left = fresh
                payload = (to_right, to_left)
                if alone is None:
                    from_left[stream] = lax.ppermute(to_right, "grp", rightward)
                    from_right[stream] = lax.ppermute(to_left, "grp", leftward)
                else:
                    outer = [(0, 1), (groups - 1, groups - 2)]
                    ends = [(groups - 2, groups - 1), (1, 0)]
                    came = lax.ppermute(alone, "grp", outer if turn == 0 else ends)
                    from_left[stream] = from_right[stream] = came
                slot = in_turn // 2
                if in_turn % 2 == 0 and slot < STREAMS and turn < turns and order[slot][turn] != 0:
                    transit.append((tick + 2,) + fetch(order[slot][turn]))
                slot = slot - STREAMS if turn < turns else slot
                if in_turn % 2 == 0 and 0 <= slot < STREAMS and turn > 0 and order[slot][turn - 1] != 0:
                    transit.append((tick + 2,) + deliver(order[slot][turn - 1]))
                if phase == groups:
                    arrived_left[stream], arrived_right[stream] = [], []
                arrived_left[stream].append(from_left[stream])
                arrived_right[stream].append(from_right[stream])
                if len(arrived_left[stream]) == groups - 1 and turn > 0:
                    for hop in range(groups - 1):
                        fresh = jnp.where(
                            group > hop,
                            arrived_left[stream][hop],
                            arrived_right[stream][groups - 2 - hop],
                        )
                        owner = lax.rem(group + groups - 1 - hop, groups)
                        new_weights = write_weights(new_weights, owner, order[stream][turn - 1], fresh)
    for _, _, step, parts in transit:
        new_held = land(new_held, step, parts)
    return (new_weights.reshape(start_weights.shape), new_held.reshape(momentum.shape))


def solution(mesh):
    in_specs = (
        P("grp", None, "shard", "tp"),
        P(None, "shard", "tp"),
        P(None, None, None, ("grp", "shard", "tp"), None, None),
    )
    out_specs = (P(None, "shard", "tp"), P(None, None, None, ("grp", "shard", "tp"), None, None))
    return jax.shard_map(body, mesh=mesh, in_specs=in_specs, out_specs=out_specs, check_vma=False)
```

```python
import jax
import jax.numpy as jnp
from jax import lax
from jax.experimental import pallas as pl
from jax.sharding import PartitionSpec as P

OUTER_RATE = 0.7
MOMENTUM_COEF = 0.5
STEPS = 8


def blank(shape):
    return pl.pallas_call(
        lambda out: None,
        out_shape=jax.ShapeDtypeStruct(shape, jnp.float32),
        out_specs=pl.BlockSpec(memory_space=pl.ANY),
    )()


def body(inner_weights, start_weights, momentum):
    groups = lax.axis_size("grp")
    shards = lax.axis_size("shard")
    tp_size = lax.axis_size("tp")
    plane = shards * tp_size
    group = lax.axis_index("grp")
    place = lax.axis_index(("shard", "tp"))
    row_count, col_count = start_weights.shape[1:]
    q_rows = row_count // (groups * plane)
    steps = min(STEPS, plane)
    merge = plane // steps
    block = (q_rows, col_count)

    inner = inner_weights.reshape((2, groups, plane) + block)
    start = start_weights.reshape((2, groups, plane) + block)
    held = momentum.reshape((2, plane) + block)
    rightward = [(i, i + 1) for i in range(groups - 1)]
    leftward = [(i + 1, i) for i in range(groups - 1)]

    def lane(shift):
        return lax.rem(place + shift, plane)

    def shifts_of(step):
        return [step * merge + m for m in range(merge)]

    def join(parts):
        return parts[0] if len(parts) == 1 else jnp.concatenate(parts, axis=0)

    def rows_of(array, matrix, owner, step):
        def cut(shift):
            return lax.dynamic_slice(array, (matrix, owner, lane(shift), 0, 0), (1, 1, 1) + block).reshape(block)

        return join([cut(shift) for shift in shifts_of(step)])

    def own(matrix, owner, step):
        return rows_of(start, matrix, owner, step) - rows_of(inner, matrix, owner, step)

    def rotate(part, shift):
        if shift % plane == 0:
            return part
        return lax.ppermute(part, ("shard", "tp"), [(i, (i + shift) % plane) for i in range(plane)])

    new_weights = blank(start.shape)
    new_held = blank(held.shape)

    def write_weights(array, matrix, owner, step, value):
        for m, shift in enumerate(shifts_of(step)):
            part = value[m * q_rows : (m + 1) * q_rows]
            array = lax.dynamic_update_slice(array, part[None, None, None], (matrix, owner, lane(shift), 0, 0))
        return array

    def after(first, *arrays):
        return lax.optimization_barrier((*first, *arrays))[len(first) :]

    order = [(turn + 1) % steps for turn in range(steps)]
    zero = jnp.zeros((merge * q_rows, col_count), jnp.float32)
    from_left, from_right = [zero, zero], [zero, zero]
    arrived_left, arrived_right = [[], []], [[], []]
    moved, outgoing, transit = {}, {}, []
    payload = (zero,)

    def fetch(step):
        (here,) = after(payload, place)
        parts = []
        for shift in shifts_of(step):
            at = lax.rem(here + plane - shift, plane)
            halves = [lax.dynamic_slice(held, (matrix, at, 0, 0), (1, 1) + block)[0] for matrix in range(2)]
            parts.append(jnp.stack([half[0] for half in halves]))
        return ("fetch", step, [rotate(part, -shift) for part, shift in zip(parts, shifts_of(step))])

    def deliver(step):
        halves = after(payload, *outgoing[step])
        parts = []
        for m, shift in enumerate(shifts_of(step)):
            parts.append(jnp.stack([half[m * q_rows : (m + 1) * q_rows] for half in halves]))
        return ("deliver", step, [rotate(part, shift) for part, shift in zip(parts, shifts_of(step))])

    def land(array, step, parts):
        for shift, part in zip(shifts_of(step), parts):
            array = lax.dynamic_update_slice(array, part[:, None], (0, lane(plane - shift), 0, 0))
        return array

    for turn in range(steps + 1):
        for phase in range(1, groups + 1):
            if turn == steps and phase > groups - 2:
                break
            for matrix in range(2):
                in_turn = (phase - 1) * 2 + matrix
                tick = turn * groups * 2 + in_turn
                landed = [entry for entry in transit if entry[0] <= tick]
                transit = [entry for entry in transit if entry[0] > tick]
                values = after(payload, from_left[matrix], from_right[matrix], *[p for e in landed for p in e[3]])
                here_left, here_right, values = values[0], values[1], list(values[2:])
                for _, kind, step, parts in landed:
                    parts, values = values[: len(parts)], values[len(parts) :]
                    if kind == "fetch":
                        moved[step] = parts
                    else:
                        new_held = land(new_held, step, parts)
                step = order[turn] if turn < steps else None
                alone = None
                if turn == 0 and phase == 1:
                    (owner,) = after(payload, jnp.where(group == 0, groups - 1, 0))
                    alone = own(matrix, owner, step)
                    to_right = to_left = alone
                elif turn == steps and phase == groups - 2:
                    alone = jnp.where(group >= groups // 2, here_left, here_right)
                    to_right = to_left = alone
                elif phase < groups:
                    to_right, to_left = here_left, here_right
                    if turn < steps:
                        right_owner = jnp.minimum(groups - phase + group, groups - 1)
                        left_owner = jnp.maximum(group - (groups - phase), 0)
                        to_right = jnp.where(group < phase, to_right + own(matrix, right_owner, step), to_right)
                        to_left = jnp.where(groups - 1 - group < phase, to_left + own(matrix, left_owner, step), to_left)
                else:
                    total = own(matrix, group, step) + here_left + here_right
                    mean_diff = total / groups
                    old_momentum = join([part[matrix] for part in moved[step]])
                    new_momentum = MOMENTUM_COEF * old_momentum + mean_diff
                    update = OUTER_RATE * (mean_diff + MOMENTUM_COEF * new_momentum)
                    outgoing.setdefault(step, []).append(new_momentum)
                    fresh = rows_of(start, matrix, group, step) - update
                    new_weights = write_weights(new_weights, matrix, group, step, fresh)
                    to_right = to_left = fresh
                payload = (to_right, to_left)
                if alone is None:
                    from_left[matrix] = lax.ppermute(to_right, "grp", rightward)
                    from_right[matrix] = lax.ppermute(to_left, "grp", leftward)
                else:
                    outer = [(0, 1), (groups - 1, groups - 2)]
                    ends = [(groups - 2, groups - 1), (1, 0)]
                    from_left[matrix] = from_right[matrix] = lax.ppermute(alone, "grp", outer if turn == 0 else ends)
                if tick == 0:
                    transit.append((tick + groups,) + fetch(order[0]))
                if in_turn == 2 * groups - 2 and turn + 1 < steps:
                    transit.append((tick + groups,) + fetch(order[turn + 1]))
                if in_turn == groups - 2 and 0 < turn < steps:
                    transit.append((tick + groups,) + deliver(order[turn - 1]))
                if phase == groups:
                    arrived_left[matrix], arrived_right[matrix] = [], []
                arrived_left[matrix].append(from_left[matrix])
                arrived_right[matrix].append(from_right[matrix])
                if len(arrived_left[matrix]) == groups - 1 and turn > 0:
                    for hop in range(groups - 1):
                        fresh = jnp.where(
                            group > hop,
                            arrived_left[matrix][hop],
                            arrived_right[matrix][groups - 2 - hop],
                        )
                        owner = lax.rem(group + groups - 1 - hop, groups)
                        new_weights = write_weights(new_weights, matrix, owner, order[turn - 1], fresh)
    new_held = land(new_held, *deliver(order[-1])[1:])
    return (new_weights.reshape(start_weights.shape), new_held.reshape(momentum.shape))


def solution(mesh):
    in_specs = (
        P("grp", None, "shard", "tp"),
        P(None, "shard", "tp"),
        P(None, None, None, ("grp", "shard", "tp"), None, None),
    )
    out_specs = (P(None, "shard", "tp"), P(None, None, None, ("grp", "shard", "tp"), None, None))
    return jax.shard_map(body, mesh=mesh, in_specs=in_specs, out_specs=out_specs, check_vma=False)
```

```python
import jax
import jax.numpy as jnp
from jax import lax
from jax.experimental import pallas as pl
from jax.experimental.pallas import tpu as pltpu
from jax.sharding import PartitionSpec as P

OUTER_RATE = 0.7
MOMENTUM_COEF = 0.5
STEPS = 8


def blank(shape):
    return pl.pallas_call(
        lambda out: None,
        out_shape=jax.ShapeDtypeStruct(shape, jnp.float32),
        out_specs=pl.BlockSpec(memory_space=pl.ANY),
    )()


def put_rows(array, matrix, group, lanes, own, from_left, from_right):
    groups = array.shape[1]
    hops = groups - 1
    q_rows = array.shape[3]

    def kernel(scalars, own, *rest):
        left, right, out, sems = rest[:hops], rest[hops : 2 * hops], rest[2 * hops + 1], rest[2 * hops + 2]
        group = scalars[0]

        def copies(source, owner, slot):
            return [
                pltpu.make_async_copy(
                    source.at[pl.ds(m * q_rows, q_rows)], out.at[matrix, owner, scalars[1 + m]], sems.at[slot, m]
                )
                for m in range(len(lanes))
            ]

        for copy in copies(own, group, hops):
            copy.start()
        for hop in range(hops):
            owner = lax.rem(group + hops - hop, groups)

            @pl.when(group > hop)
            def _():
                for copy in copies(left[hop], owner, hop):
                    copy.start()

            @pl.when(group <= hop)
            def _():
                for copy in copies(right[hops - 1 - hop], owner, hop):
                    copy.start()

        for slot in range(groups):
            for copy in copies(own, group, slot):
                copy.wait()

    anywhere = pl.BlockSpec(memory_space=pl.ANY)
    size = own.size * 4
    return pl.pallas_call(
        kernel,
        out_shape=jax.ShapeDtypeStruct(array.shape, array.dtype),
        in_specs=[pl.BlockSpec(memory_space=pltpu.SMEM)] + [anywhere] * (2 * groups),
        out_specs=anywhere,
        scratch_shapes=[pltpu.SemaphoreType.DMA((groups, len(lanes)))],
        input_output_aliases={2 * groups: 0},
        cost_estimate=pl.CostEstimate(flops=0, bytes_accessed=2 * groups * size, transcendentals=0),
    )(jnp.stack([group, *lanes]).astype(jnp.int32), own, *from_left, *from_right, array)


def body(inner_weights, start_weights, momentum):
    groups = lax.axis_size("grp")
    shards = lax.axis_size("shard")
    tp_size = lax.axis_size("tp")
    plane = shards * tp_size
    group = lax.axis_index("grp")
    place = lax.axis_index(("shard", "tp"))
    row_count, col_count = start_weights.shape[1:]
    q_rows = row_count // (groups * plane)
    steps = min(STEPS, plane)
    merge = plane // steps
    block = (q_rows, col_count)

    inner = inner_weights.reshape((2, groups, plane) + block)
    start = start_weights.reshape((2, groups, plane) + block)
    held = momentum.reshape((2, plane) + block)
    rightward = [(i, i + 1) for i in range(groups - 1)]
    leftward = [(i + 1, i) for i in range(groups - 1)]

    def lane(shift):
        return lax.rem(place + shift, plane)

    def shifts_of(step):
        return [step * merge + m for m in range(merge)]

    def join(parts):
        return parts[0] if len(parts) == 1 else jnp.concatenate(parts, axis=0)

    def rows_of(array, matrix, owner, step):
        def cut(shift):
            return lax.dynamic_slice(array, (matrix, owner, lane(shift), 0, 0), (1, 1, 1) + block).reshape(block)

        return join([cut(shift) for shift in shifts_of(step)])

    def own(matrix, owner, step):
        return rows_of(start, matrix, owner, step) - rows_of(inner, matrix, owner, step)

    def rotate(part, shift):
        if shift % plane == 0:
            return part
        return lax.ppermute(part, ("shard", "tp"), [(i, (i + shift) % plane) for i in range(plane)])

    new_weights = blank(start.shape)
    new_held = blank(held.shape)

    def after(first, *arrays):
        return lax.optimization_barrier((*first, *arrays))[len(first) :]

    order = [(turn + 1) % steps for turn in range(steps)]
    zero = jnp.zeros((merge * q_rows, col_count), jnp.float32)
    from_left, from_right = [zero, zero], [zero, zero]
    arrived_left, arrived_right = [[], []], [[], []]
    kept, moved, outgoing, transit = [None, None], {}, {}, []
    payload = (zero,)

    def fetch(step):
        (here,) = after(payload, place)
        parts = []
        for shift in shifts_of(step):
            at = lax.rem(here + plane - shift, plane)
            halves = [lax.dynamic_slice(held, (matrix, at, 0, 0), (1, 1) + block)[0] for matrix in range(2)]
            parts.append(jnp.stack([half[0] for half in halves]))
        return ("fetch", step, [rotate(part, -shift) for part, shift in zip(parts, shifts_of(step))])

    def deliver(step):
        halves = after(payload, *outgoing[step])
        parts = []
        for m, shift in enumerate(shifts_of(step)):
            parts.append(jnp.stack([half[m * q_rows : (m + 1) * q_rows] for half in halves]))
        return ("deliver", step, [rotate(part, shift) for part, shift in zip(parts, shifts_of(step))])

    def land(array, step, parts):
        for shift, part in zip(shifts_of(step), parts):
            array = lax.dynamic_update_slice(array, part[:, None], (0, lane(plane - shift), 0, 0))
        return array

    for turn in range(steps + 1):
        for phase in range(1, groups + 1):
            if turn == steps and phase > groups - 2:
                break
            for matrix in range(2):
                in_turn = (phase - 1) * 2 + matrix
                tick = turn * groups * 2 + in_turn
                landed = [entry for entry in transit if entry[0] <= tick]
                transit = [entry for entry in transit if entry[0] > tick]
                values = after(payload, from_left[matrix], from_right[matrix], *[p for e in landed for p in e[3]])
                here_left, here_right, values = values[0], values[1], list(values[2:])
                for _, kind, step, parts in landed:
                    parts, values = values[: len(parts)], values[len(parts) :]
                    if kind == "fetch":
                        moved[step] = parts
                    else:
                        new_held = land(new_held, step, parts)
                step = order[turn] if turn < steps else None
                alone = None
                if turn == 0 and phase == 1:
                    (owner,) = after(payload, jnp.where(group == 0, groups - 1, 0))
                    alone = own(matrix, owner, step)
                    to_right = to_left = alone
                elif turn == steps and phase == groups - 2:
                    alone = jnp.where(group >= groups // 2, here_left, here_right)
                    to_right = to_left = alone
                elif phase < groups:
                    to_right, to_left = here_left, here_right
                    if turn < steps:
                        right_owner = jnp.minimum(groups - phase + group, groups - 1)
                        left_owner = jnp.maximum(group - (groups - phase), 0)
                        to_right = jnp.where(group < phase, to_right + own(matrix, right_owner, step), to_right)
                        to_left = jnp.where(groups - 1 - group < phase, to_left + own(matrix, left_owner, step), to_left)
                else:
                    total = own(matrix, group, step) + here_left + here_right
                    mean_diff = total / groups
                    old_momentum = join([part[matrix] for part in moved[step]])
                    new_momentum = MOMENTUM_COEF * old_momentum + mean_diff
                    update = OUTER_RATE * (mean_diff + MOMENTUM_COEF * new_momentum)
                    outgoing.setdefault(step, []).append(new_momentum)
                    kept[matrix] = rows_of(start, matrix, group, step) - update
                    to_right = to_left = kept[matrix]
                payload = (to_right, to_left)
                if alone is None:
                    from_left[matrix] = lax.ppermute(to_right, "grp", rightward)
                    from_right[matrix] = lax.ppermute(to_left, "grp", leftward)
                else:
                    outer = [(0, 1), (groups - 1, groups - 2)]
                    ends = [(groups - 2, groups - 1), (1, 0)]
                    from_left[matrix] = from_right[matrix] = lax.ppermute(alone, "grp", outer if turn == 0 else ends)
                if in_turn == 0 and turn < steps:
                    transit.append((tick + 3,) + fetch(order[turn]))
                if in_turn == 3 and 0 < turn < steps:
                    transit.append((tick + 5,) + deliver(order[turn - 1]))
                if phase == groups:
                    arrived_left[matrix], arrived_right[matrix] = [], []
                arrived_left[matrix].append(from_left[matrix])
                arrived_right[matrix].append(from_right[matrix])
                if len(arrived_left[matrix]) == groups - 1 and turn > 0:
                    lanes = [lane(shift) for shift in shifts_of(order[turn - 1])]
                    new_weights = put_rows(
                        new_weights, matrix, group, lanes, kept[matrix], arrived_left[matrix], arrived_right[matrix]
                    )
    new_held = land(new_held, *deliver(order[-1])[1:])
    return (new_weights.reshape(start_weights.shape), new_held.reshape(momentum.shape))


def solution(mesh):
    in_specs = (
        P("grp", None, "shard", "tp"),
        P(None, "shard", "tp"),
        P(None, None, None, ("grp", "shard", "tp"), None, None),
    )
    out_specs = (P(None, "shard", "tp"), P(None, None, None, ("grp", "shard", "tp"), None, None))
    return jax.shard_map(body, mesh=mesh, in_specs=in_specs, out_specs=out_specs, check_vma=False)
```

```python
import jax
import jax.numpy as jnp
from jax import lax
from jax.experimental import pallas as pl
from jax.experimental.pallas import tpu as pltpu
from jax.sharding import PartitionSpec as P

OUTER_RATE = 0.7
MOMENTUM_COEF = 0.5
STEPS = 8


def blank(shape):
    return pl.pallas_call(
        lambda out: None,
        out_shape=jax.ShapeDtypeStruct(shape, jnp.float32),
        out_specs=pl.BlockSpec(memory_space=pl.ANY),
    )()


def put_rows(array, matrix, group, lanes, own, from_left, from_right):
    groups = array.shape[1]
    hops = groups - 1
    parts = [part.reshape((len(lanes),) + array.shape[3:]) for part in (own, *from_left, *from_right)]

    def kernel(scalars, own, *rest):
        left, right = rest[:hops], rest[hops : 2 * hops]
        out, stage, read, written = rest[2 * hops + 1 :]
        group = scalars[0]

        def load(source, slot):
            return pltpu.make_async_copy(source, stage.at[slot], read.at[slot])

        def stores(slot):
            owner = group if slot == hops else lax.rem(group + hops - slot, groups)
            return [
                pltpu.make_async_copy(stage.at[slot, m], out.at[matrix, owner, scalars[1 + m]], written.at[slot, m])
                for m in range(len(lanes))
            ]

        load(own, hops).start()
        for hop in range(hops):

            @pl.when(group > hop)
            def _():
                load(left[hop], hop).start()

            @pl.when(group <= hop)
            def _():
                load(right[hops - 1 - hop], hop).start()

        order = [hops, *range(hops)]
        for slot in order:
            load(own, slot).wait()
            for store in stores(slot):
                store.start()
        for slot in order:
            for store in stores(slot):
                store.wait()

    anywhere = pl.BlockSpec(memory_space=pl.ANY)
    size = own.size * 4
    return pl.pallas_call(
        kernel,
        out_shape=jax.ShapeDtypeStruct(array.shape, array.dtype),
        in_specs=[pl.BlockSpec(memory_space=pltpu.SMEM)] + [anywhere] * (2 * groups),
        out_specs=anywhere,
        scratch_shapes=[
            pltpu.VMEM((groups, len(lanes)) + array.shape[3:], array.dtype),
            pltpu.SemaphoreType.DMA((groups,)),
            pltpu.SemaphoreType.DMA((groups, len(lanes))),
        ],
        input_output_aliases={2 * groups: 0},
        cost_estimate=pl.CostEstimate(flops=0, bytes_accessed=2 * groups * size, transcendentals=0),
    )(jnp.stack([group, *lanes]).astype(jnp.int32), *parts, array)


def body(inner_weights, start_weights, momentum):
    groups = lax.axis_size("grp")
    shards = lax.axis_size("shard")
    tp_size = lax.axis_size("tp")
    plane = shards * tp_size
    group = lax.axis_index("grp")
    place = lax.axis_index(("shard", "tp"))
    row_count, col_count = start_weights.shape[1:]
    q_rows = row_count // (groups * plane)
    steps = min(STEPS, plane)
    merge = plane // steps
    block = (q_rows, col_count)

    inner = inner_weights.reshape((2, groups, plane) + block)
    start = start_weights.reshape((2, groups, plane) + block)
    held = momentum.reshape((2, plane) + block)
    rightward = [(i, i + 1) for i in range(groups - 1)]
    leftward = [(i + 1, i) for i in range(groups - 1)]

    def lane(shift):
        return lax.rem(place + shift, plane)

    def shifts_of(step):
        return [step * merge + m for m in range(merge)]

    def join(parts):
        return parts[0] if len(parts) == 1 else jnp.concatenate(parts, axis=0)

    def rows_of(array, matrix, owner, step):
        def cut(shift):
            return lax.dynamic_slice(array, (matrix, owner, lane(shift), 0, 0), (1, 1, 1) + block).reshape(block)

        return join([cut(shift) for shift in shifts_of(step)])

    def own(matrix, owner, step):
        return rows_of(start, matrix, owner, step) - rows_of(inner, matrix, owner, step)

    def rotate(part, shift):
        if shift % plane == 0:
            return part
        return lax.ppermute(part, ("shard", "tp"), [(i, (i + shift) % plane) for i in range(plane)])

    new_weights = blank(start.shape)
    new_held = blank(held.shape)

    def after(first, *arrays):
        return lax.optimization_barrier((*first, *arrays))[len(first) :]

    order = [(turn + 1) % steps for turn in range(steps)]
    zero = jnp.zeros((merge * q_rows, col_count), jnp.float32)
    from_left, from_right = [zero, zero], [zero, zero]
    arrived_left, arrived_right = [[], []], [[], []]
    kept, moved, outgoing, transit = [None, None], {}, {}, []
    payload = (zero,)

    def fetch(step):
        (here,) = after(payload, place)
        parts = []
        for shift in shifts_of(step):
            at = lax.rem(here + plane - shift, plane)
            halves = [lax.dynamic_slice(held, (matrix, at, 0, 0), (1, 1) + block)[0] for matrix in range(2)]
            parts.append(jnp.stack([half[0] for half in halves]))
        return ("fetch", step, [rotate(part, -shift) for part, shift in zip(parts, shifts_of(step))])

    def deliver(step):
        halves = after(payload, *outgoing[step])
        parts = []
        for m, shift in enumerate(shifts_of(step)):
            parts.append(jnp.stack([half[m * q_rows : (m + 1) * q_rows] for half in halves]))
        return ("deliver", step, [rotate(part, shift) for part, shift in zip(parts, shifts_of(step))])

    def land(array, step, parts):
        for shift, part in zip(shifts_of(step), parts):
            array = lax.dynamic_update_slice(array, part[:, None], (0, lane(plane - shift), 0, 0))
        return array

    for turn in range(steps + 1):
        for phase in range(1, groups + 1):
            if turn == steps and phase > groups - 2:
                break
            for matrix in range(2):
                in_turn = (phase - 1) * 2 + matrix
                tick = turn * groups * 2 + in_turn
                landed = [entry for entry in transit if entry[0] <= tick]
                transit = [entry for entry in transit if entry[0] > tick]
                values = after(payload, from_left[matrix], from_right[matrix], *[p for e in landed for p in e[3]])
                here_left, here_right, values = values[0], values[1], list(values[2:])
                for _, kind, step, parts in landed:
                    parts, values = values[: len(parts)], values[len(parts) :]
                    if kind == "fetch":
                        moved[step] = parts
                    else:
                        new_held = land(new_held, step, parts)
                step = order[turn] if turn < steps else None
                alone = None
                if turn == 0 and phase == 1:
                    (owner,) = after(payload, jnp.where(group == 0, groups - 1, 0))
                    alone = own(matrix, owner, step)
                    to_right = to_left = alone
                elif turn == steps and phase == groups - 2:
                    alone = jnp.where(group >= groups // 2, here_left, here_right)
                    to_right = to_left = alone
                elif phase < groups:
                    to_right, to_left = here_left, here_right
                    if turn < steps:
                        right_owner = jnp.minimum(groups - phase + group, groups - 1)
                        left_owner = jnp.maximum(group - (groups - phase), 0)
                        to_right = jnp.where(group < phase, to_right + own(matrix, right_owner, step), to_right)
                        to_left = jnp.where(groups - 1 - group < phase, to_left + own(matrix, left_owner, step), to_left)
                else:
                    total = own(matrix, group, step) + here_left + here_right
                    mean_diff = total / groups
                    old_momentum = join([part[matrix] for part in moved[step]])
                    new_momentum = MOMENTUM_COEF * old_momentum + mean_diff
                    update = OUTER_RATE * (mean_diff + MOMENTUM_COEF * new_momentum)
                    outgoing.setdefault(step, []).append(new_momentum)
                    kept[matrix] = rows_of(start, matrix, group, step) - update
                    to_right = to_left = kept[matrix]
                payload = (to_right, to_left)
                if alone is None:
                    from_left[matrix] = lax.ppermute(to_right, "grp", rightward)
                    from_right[matrix] = lax.ppermute(to_left, "grp", leftward)
                else:
                    outer = [(0, 1), (groups - 1, groups - 2)]
                    ends = [(groups - 2, groups - 1), (1, 0)]
                    from_left[matrix] = from_right[matrix] = lax.ppermute(alone, "grp", outer if turn == 0 else ends)
                if in_turn == 0 and turn < steps:
                    transit.append((tick + 3,) + fetch(order[turn]))
                if in_turn == 3 and 0 < turn < steps:
                    transit.append((tick + 5,) + deliver(order[turn - 1]))
                if phase == groups:
                    arrived_left[matrix], arrived_right[matrix] = [], []
                arrived_left[matrix].append(from_left[matrix])
                arrived_right[matrix].append(from_right[matrix])
                if len(arrived_left[matrix]) == groups - 1 and turn > 0:
                    lanes = [lane(shift) for shift in shifts_of(order[turn - 1])]
                    new_weights = put_rows(
                        new_weights, matrix, group, lanes, kept[matrix], arrived_left[matrix], arrived_right[matrix]
                    )
    new_held = land(new_held, *deliver(order[-1])[1:])
    return (new_weights.reshape(start_weights.shape), new_held.reshape(momentum.shape))


def solution(mesh):
    in_specs = (
        P("grp", None, "shard", "tp"),
        P(None, "shard", "tp"),
        P(None, None, None, ("grp", "shard", "tp"), None, None),
    )
    out_specs = (P(None, "shard", "tp"), P(None, None, None, ("grp", "shard", "tp"), None, None))
    return jax.shard_map(body, mesh=mesh, in_specs=in_specs, out_specs=out_specs, check_vma=False)
```

```python
import jax
import jax.numpy as jnp
from jax import lax
from jax.experimental import pallas as pl
from jax.sharding import PartitionSpec as P

OUTER_RATE = 0.7
MOMENTUM_COEF = 0.5
STEPS = 8


def blank(shape):
    return pl.pallas_call(
        lambda out: None,
        out_shape=jax.ShapeDtypeStruct(shape, jnp.float32),
        out_specs=pl.BlockSpec(memory_space=pl.ANY),
    )()


def body(inner_weights, start_weights, momentum):
    groups = lax.axis_size("grp")
    shards = lax.axis_size("shard")
    tp_size = lax.axis_size("tp")
    plane = shards * tp_size
    group = lax.axis_index("grp")
    place = lax.axis_index(("shard", "tp"))
    row_count, col_count = start_weights.shape[1:]
    q_rows = row_count // (groups * plane)
    steps = min(STEPS, plane)
    merge = plane // steps
    block = (q_rows, col_count)

    inner = inner_weights.reshape((2, groups, plane) + block)
    start = start_weights.reshape((2, groups, plane) + block)
    held = momentum.reshape((2, plane) + block)
    rightward = [(i, i + 1) for i in range(groups - 1)]
    leftward = [(i + 1, i) for i in range(groups - 1)]

    def lane(shift):
        return lax.rem(place + shift, plane)

    def shifts_of(step):
        return [step * merge + m for m in range(merge)]

    def join(parts):
        return parts[0] if len(parts) == 1 else jnp.concatenate(parts, axis=0)

    def rows_of(array, matrix, owner, step):
        def cut(shift):
            return lax.dynamic_slice(array, (matrix, owner, lane(shift), 0, 0), (1, 1, 1) + block).reshape(block)

        return join([cut(shift) for shift in shifts_of(step)])

    def own(matrix, owner, step):
        return rows_of(start, matrix, owner, step) - rows_of(inner, matrix, owner, step)

    def rotate(part, shift):
        if shift % plane == 0:
            return part
        return lax.ppermute(part, ("shard", "tp"), [(i, (i + shift) % plane) for i in range(plane)])

    new_weights = blank(start.shape)
    new_held = blank(held.shape)

    def write_weights(array, matrix, owner, step, value):
        for m, shift in enumerate(shifts_of(step)):
            part = value[m * q_rows : (m + 1) * q_rows]
            array = lax.dynamic_update_slice(array, part[None, None, None], (matrix, owner, lane(shift), 0, 0))
        return array

    def after(first, *arrays):
        return lax.optimization_barrier((*first, *arrays))[len(first) :]

    order = [(turn + 1) % steps for turn in range(steps)]
    zero = jnp.zeros((merge * q_rows, col_count), jnp.float32)
    from_left, from_right = [zero, zero], [zero, zero]
    arrived_left, arrived_right = [[], []], [[], []]
    moved, outgoing, transit = {}, {}, []
    payload = (zero,)

    def fetch(step):
        (here,) = after(payload, place)
        parts = []
        for shift in shifts_of(step):
            at = lax.rem(here + plane - shift, plane)
            halves = [lax.dynamic_slice(held, (matrix, at, 0, 0), (1, 1) + block)[0] for matrix in range(2)]
            parts.append(jnp.stack([half[0] for half in halves]))
        return ("fetch", step, [rotate(part, -shift) for part, shift in zip(parts, shifts_of(step))])

    def deliver(step):
        halves = after(payload, *outgoing[step])
        parts = []
        for m, shift in enumerate(shifts_of(step)):
            parts.append(jnp.stack([half[m * q_rows : (m + 1) * q_rows] for half in halves]))
        return ("deliver", step, [rotate(part, shift) for part, shift in zip(parts, shifts_of(step))])

    def land(array, step, parts):
        for shift, part in zip(shifts_of(step), parts):
            array = lax.dynamic_update_slice(array, part[:, None], (0, lane(plane - shift), 0, 0))
        return array

    for turn in range(steps + 1):
        for phase in range(1, groups + 1):
            if turn == steps and phase > groups - 2:
                break
            for matrix in range(2):
                in_turn = (phase - 1) * 2 + matrix
                tick = turn * groups * 2 + in_turn
                landed = [entry for entry in transit if entry[0] <= tick]
                transit = [entry for entry in transit if entry[0] > tick]
                values = after(payload, from_left[matrix], from_right[matrix], *[p for e in landed for p in e[3]])
                here_left, here_right, values = values[0], values[1], list(values[2:])
                for _, kind, step, parts in landed:
                    parts, values = values[: len(parts)], values[len(parts) :]
                    if kind == "fetch":
                        moved[step] = parts
                    else:
                        new_held = land(new_held, step, parts)
                step = order[turn] if turn < steps else None
                alone = None
                if turn == 0 and phase == 1:
                    (owner,) = after(payload, jnp.where(group == 0, groups - 1, 0))
                    alone = own(matrix, owner, step)
                    to_right = to_left = alone
                elif turn == steps and phase == groups - 2:
                    alone = jnp.where(group >= groups // 2, here_left, here_right)
                    to_right = to_left = alone
                elif phase < groups:
                    to_right, to_left = here_left, here_right
                    if turn < steps:
                        right_owner = jnp.minimum(groups - phase + group, groups - 1)
                        left_owner = jnp.maximum(group - (groups - phase), 0)
                        to_right = jnp.where(group < phase, to_right + own(matrix, right_owner, step), to_right)
                        to_left = jnp.where(groups - 1 - group < phase, to_left + own(matrix, left_owner, step), to_left)
                else:
                    total = own(matrix, group, step) + here_left + here_right
                    mean_diff = total / groups
                    old_momentum = join([part[matrix] for part in moved[step]])
                    new_momentum = MOMENTUM_COEF * old_momentum + mean_diff
                    update = OUTER_RATE * (mean_diff + MOMENTUM_COEF * new_momentum)
                    outgoing.setdefault(step, []).append(new_momentum)
                    fresh = rows_of(start, matrix, group, step) - update
                    new_weights = write_weights(new_weights, matrix, group, step, fresh)
                    to_right = to_left = fresh
                payload = (to_right, to_left)
                if alone is None:
                    from_left[matrix] = lax.ppermute(to_right, "grp", rightward)
                    from_right[matrix] = lax.ppermute(to_left, "grp", leftward)
                else:
                    outer = [(0, 1), (groups - 1, groups - 2)]
                    ends = [(groups - 2, groups - 1), (1, 0)]
                    from_left[matrix] = from_right[matrix] = lax.ppermute(alone, "grp", outer if turn == 0 else ends)
                if in_turn == 0 and turn < steps:
                    transit.append((tick + 3,) + fetch(order[turn]))
                if in_turn == 3 and 0 < turn < steps:
                    transit.append((tick + 5,) + deliver(order[turn - 1]))
                if phase == groups:
                    arrived_left[matrix], arrived_right[matrix] = [], []
                arrived_left[matrix].append(from_left[matrix])
                arrived_right[matrix].append(from_right[matrix])
                if len(arrived_left[matrix]) == groups - 1 and turn > 0:
                    for hop in range(groups - 1):
                        fresh = jnp.where(
                            group > hop,
                            arrived_left[matrix][hop],
                            arrived_right[matrix][groups - 2 - hop],
                        )
                        owner = lax.rem(group + groups - 1 - hop, groups)
                        new_weights = write_weights(new_weights, matrix, owner, order[turn - 1], fresh)
    new_held = land(new_held, *deliver(order[-1])[1:])
    return (new_weights.reshape(start_weights.shape), new_held.reshape(momentum.shape))


def solution(mesh):
    in_specs = (
        P("grp", None, "shard", "tp"),
        P(None, "shard", "tp"),
        P(None, None, None, ("grp", "shard", "tp"), None, None),
    )
    out_specs = (P(None, "shard", "tp"), P(None, None, None, ("grp", "shard", "tp"), None, None))
    return jax.shard_map(body, mesh=mesh, in_specs=in_specs, out_specs=out_specs, check_vma=False)
```
